256 devices in a mesh: tour: 16 (over z_hi, x), team: 16 (over y, z_lo, core).
Axes of the slice: x: 4, y: 4, z: 8 (z_hi: 4, z_lo: 2; z = z_hi * 2 + z_lo), core: 2. Of those that a mesh axis runs over, the one named last changes fastest.
Arguments:
- embeddings: float32 [65536, 128], P(('tour', 'team')), may hold values from -120 to 120
Outputs:
- embedding_grad: float32 [65536, 128], P(('tour', 'team'))
- uniformity_loss: float32 [], replicated
The draws below stay inside these ranges and needn't reach their ends.
All inputs are finite; a program needn't handle non-finite values.
Results may differ from the reference program's by a relative error of at most 0.0012.
Values may be sent and summed in bfloat16 or wider, within the bound.
A program may use at most 128 MiB of HBM per device.

```python
import math
import jax
import jax.numpy as jnp
from jax import lax

D = 128
BLOCK = 4096
ROWS = 65536
N_TOUR = 16


def draw_embeddings(key, part):
    key = jax.random.fold_in(key, 11)
    key_center, key_ids, key_noise, key_scale = jax.random.split(key, 4)
    centers = jax.random.normal(key_center, (64, D), jnp.float32)
    position = jnp.arange(ROWS, dtype=jnp.int32)
    spread = 64 - 60 * position // ROWS
    labels = jax.random.randint(key_ids, (ROWS,), 0, 64) % spread
    strength = (0.5 + position.astype(jnp.float32) / ROWS)[:, None]
    noise = jax.random.normal(key_noise, (ROWS, D), jnp.float32)
    scales = jnp.exp(jax.random.uniform(key_scale, (ROWS, 1), jnp.float32, 0.0, math.log(10.0)))
    values = (strength * centers[labels] + noise) * scales
    return jnp.clip(values, -120.0, 120.0)


def setup_inputs(seed: int = 0) -> dict:
    key_list = jax.random.split(jax.random.key(seed), 2)
    embeddings = draw_embeddings(jax.random.fold_in(key_list[1], 71), 0)
    return {"embeddings": embeddings}


def reference(embeddings):
    squares = lax.optimization_barrier(jnp.sum(embeddings * embeddings, axis=1, keepdims=True))
    inv_norm = lax.rsqrt(squares + 1e-06)
    direction = embeddings * inv_norm
    unit = direction.astype(jnp.bfloat16)
    unit_wide = unit.astype(jnp.float32)
    self_weight = jnp.exp(4.0 * lax.optimization_barrier(jnp.sum(unit_wide * unit_wide, axis=1)) - 4.0)
    blocks = unit.reshape(N_TOUR, BLOCK, D)

    def row_pass(row_block):

        def col_pass(carried, col_block):
            scores = lax.dot_general(row_block, col_block, (((1,), (1,)), ((), ())), preferred_element_type=jnp.float32)
            weights = jnp.exp(4.0 * scores - 4.0)
            pull_sum = carried[0] + jnp.dot(weights.astype(jnp.bfloat16), col_block, preferred_element_type=jnp.float32)
            return ((pull_sum, carried[1] + jnp.sum(weights)), None)
        initial = (jnp.zeros((BLOCK, D), jnp.float32), jnp.zeros((), jnp.float32))
        result, unused = lax.scan(col_pass, initial, blocks)
        return result
    pull_blocks, sum_blocks = lax.map(row_pass, blocks)
    pair_total = jnp.sum(sum_blocks) - jnp.sum(self_weight)
    uniformity_loss = jnp.log(pair_total / (ROWS * (ROWS - 1.0)))
    pull_sum = pull_blocks.reshape(ROWS, D) - self_weight[:, None] * unit_wide
    radial = lax.optimization_barrier(jnp.sum(direction * pull_sum, axis=1, keepdims=True))
    factor = ROWS * ROWS / 8.0 / pair_total
    embedding_grad = factor * inv_norm * (pull_sum - direction * radial)
    return (embedding_grad, uniformity_loss)
```

```python
import functools
import math

import jax
import jax.numpy as jnp
from jax import lax
from jax.experimental import pallas as pl
from jax.experimental.pallas import tpu as pltpu
from jax.sharding import PartitionSpec as P

F32, BF16 = jnp.float32, jnp.bfloat16
MESH = pl.DeviceIdType.MESH
SCALE = 4.0 / math.log(2.0)
SHIFT = math.exp(-4.0)
NX, NY, NZ = 4, 4, 8
D, B = 128, 256
H = B // 2
QROWS = 2048
ORDER = (0, 1, -1, 2, -2, 3, -3, 4)
SLOT = {o: p for p, o in enumerate(ORDER)}
SLOT[-4] = SLOT[4]


def unit_at(half, core, d):
    if d == 0:
        return 0, 2 * core + half
    if d == 2:
        return 3, 2 * core + half
    return 1 + core, (0 if d == 1 else 2) + half


def dot(a, b):
    return lax.dot_general(a, b, (((1,), (0,)), ((), ())), preferred_element_type=F32)


class Net:
    def __init__(self, send, recv):
        t, m = lax.axis_index("tour"), lax.axis_index("team")
        self.z = (t // 4) * 2 + (m // 2) % 2
        self.x, self.y, self.c = t % 4, m // 4, m % 2
        self.send, self.recv = send, recv
        self.count = 0
        self.started = []

    def at(self, dx=0, dy=0, dz=0, dc=0):
        x, y = (self.x + dx) % NX, (self.y + dy) % NY
        z, c = (self.z + dz) % NZ, (self.c + dc) % 2
        return ((z // 2) * 4 + x, (y * 2 + z % 2) * 2 + c)

    def copy(self, src, dst, **where):
        i = self.count
        self.count += 1
        return pltpu.make_async_remote_copy(
            src_ref=src, dst_ref=dst, send_sem=self.send.at[i], recv_sem=self.recv.at[i],
            device_id=self.at(**where), device_id_type=MESH)


def kernel(emb_ref, out_ref, tot_ref, cols, colt, rowt, acc, w0, w1, ssum, part, got, sums, send, recv):
    net = Net(send, recv)
    line = [(dz, dc) for dz in range(NZ) for dc in range(2) if (dz, dc) != (0, 0)]
    plane = [(dx, dy) for dx in range(NX) for dy in range(NY) if (dx, dy) != (0, 0)]

    barrier = pltpu.get_barrier_semaphore()
    for dz, dc in line:
        pl.semaphore_signal(barrier, inc=1, device_id=net.at(dz=dz, dc=dc), device_id_type=MESH)
    for dx, dy in plane:
        pl.semaphore_signal(barrier, inc=1, device_id=net.at(dx=dx, dy=dy), device_id_type=MESH)

    def unit(half, core, d, n=1):
        q, i = unit_at(half, core, d)
        return cols.at[q, i] if n == 1 else cols.at[q, pl.ds(i, n)]

    first_a = [net.copy(unit(0, 0, 0).at[pl.ds(0, H)], unit(0, 0, 0).at[pl.ds((-d % 4) * H, H)], dx=d) for d in (1, 3, 2)]
    first_b = [net.copy(unit(1, 0, 0).at[pl.ds(0, H)], unit(1, 0, 0).at[pl.ds((-d % 4) * H, H)], dy=d) for d in (1, 3, 2)]
    second_a = {d: net.copy(unit(0, 0, 0), unit(0, 0, -d % 4), dy=d) for d in (1, 3, 2)}
    second_b = {d: net.copy(unit(1, 0, 0), unit(1, 0, -d % 4), dx=d) for d in (1, 3, 2)}
    sib = {d: net.copy(unit(0, 0, d, 2), unit(0, 1, d, 2), dc=1) for d in (0, 1, 3, 2)}
    up = [net.copy(rowt.at[SLOT[-k]], rowt.at[SLOT[-k - 1]], dz=1) for k in range(3)]
    down = [net.copy(rowt.at[SLOT[k]], rowt.at[SLOT[k + 1]], dz=-1) for k in range(3)]
    lo, hi = pl.ds(0, H), pl.ds(H, H)
    up.append(net.copy(rowt.at[SLOT[-3], :, lo], rowt.at[SLOT[4], :, lo], dz=1))
    down.append(net.copy(rowt.at[SLOT[3], :, hi], rowt.at[SLOT[4], :, hi], dz=-1))
    sum_up = {4: net.copy(part.at[SLOT[4], :, lo], got.at[SLOT[3], :, lo], dz=1)}
    sum_down = {4: net.copy(part.at[SLOT[4], :, hi], got.at[SLOT[-3], :, hi], dz=-1)}
    for o in (3, 2, 1):
        sum_up[o] = net.copy(part.at[SLOT[o]], got.at[SLOT[o - 1] if o > 1 else 0], dz=1)
        sum_down[o] = net.copy(part.at[SLOT[-o]], got.at[SLOT[1 - o] if o > 1 else 7], dz=-1)
    tell_line = [net.copy(sums.at[0], sums.at[1 + i], dz=dz, dc=dc) for i, (dz, dc) in enumerate(line)]
    tell_plane = [net.copy(sums.at[16], sums.at[17 + i], dx=dx, dy=dy) for i, (dx, dy) in enumerate(plane)]

    emb = emb_ref[...]
    inv_norm = lax.rsqrt(jnp.sum(emb * emb, axis=1, keepdims=True) + 1e-06)
    direction = emb * inv_norm
    own = direction.astype(BF16)
    wide = own.astype(F32)
    cols[0, 0, 0:H] = own[0:H]
    cols[0, 1, 0:H] = own[H:B]
    rowt[0] = wide.T.astype(BF16)
    acc[...] = jnp.zeros_like(acc)
    ssum[...] = jnp.zeros_like(ssum)
    pl.semaphore_wait(barrier, len(line) + len(plane))

    for c in first_a + first_b:
        c.start()
    up[0].start()
    down[0].start()

    def turn(q, i):
        colt[q, :, i * 512:(i + 1) * 512] = cols[q, i].astype(F32).T.astype(BF16)

    def scores(p, q, w):
        s = dot(cols[q].reshape(QROWS, D), rowt[p])
        e = jnp.exp2(s * SCALE)
        ssum[...] += jnp.sum(e.reshape(QROWS // 8, 8, B), axis=0)
        w[...] = e.astype(BF16)

    def pull(p, q, w):
        acc[p] += dot(colt[q], w[...])

    def place(s):
        k = s - 7
        p = jnp.where(s < 7, s + 1, jnp.where(s < 28, 7 - k // 3, 0))
        q = jnp.where(s < 7, 0, jnp.where(s < 28, 1 + k % 3, s - 28))
        return p, q

    up[0].wait_recv()
    up[1].start()
    down[0].wait_recv()
    down[1].start()
    for c in first_a:
        c.wait_recv()
    for d in (1, 3, 2):
        second_a[d].start()
    for c in first_b:
        c.wait_recv()
    for d in (1, 3, 2):
        second_b[d].start()
    sib[0].start()
    turn(0, 0)
    turn(0, 1)
    up[1].wait_recv()
    up[2].start()
    down[1].wait_recv()
    down[2].start()
    sib[0].wait_recv()
    turn(0, 2)
    turn(0, 3)

    def pass_on(o):
        p = SLOT[o]
        if abs(o) == 3:
            s = pl.ds(0, H) if o > 0 else pl.ds(H, H)
            (sum_up if o > 0 else sum_down)[4].wait_recv()
            r = pl.ds(H, H) if o > 0 else pl.ds(0, H)
            part[p, :, s] = acc[p, :, s] + got[p, :, s]
            part[p, :, r] = acc[p, :, r]
        else:
            (sum_up if o > 0 else sum_down)[abs(o) + 1].wait_recv()
            part[p] = acc[p] + got[p]
        (sum_up if o > 0 else sum_down)[abs(o)].start()

    def events(it):
        @pl.when(it == 1)
        def _():
            up[2].wait_recv()
            up[3].start()
            down[2].wait_recv()
            down[3].start()

        @pl.when(it == 2)
        def _():
            up[3].wait_recv()
            down[3].wait_recv()
            for d in (1, 3):
                second_a[-d % 4].wait_recv()
                second_b[-d % 4].wait_recv()
                sib[d].start()
            for i in range(4):
                turn(1, i)

        @pl.when(it == 3)
        def _():
            second_a[2].wait_recv()
            second_b[2].wait_recv()
            sib[2].start()
            sib[1].wait_recv()
            sib[3].wait_recv()
            for i in range(4):
                turn(2, i)

        @pl.when(it == 4)
        def _():
            sib[2].wait_recv()
            for i in range(4):
                turn(3, i)

        @pl.when(it == 5)
        def _():
            part[SLOT[4]] = acc[SLOT[4]]
            sum_up[4].start()
            sum_down[4].start()

        for k, o in ((1, -3), (2, 3), (3, -2), (4, 2), (5, -1), (6, 1)):
            @pl.when(it == (9 + 3 * k) // 2 + 1)
            def _(o=o):
                pass_on(o)

    scores(*place(0), w0)

    @pl.loop(0, 15)
    def _(it):
        events(it)
        here, there, after = place(2 * it), place(2 * it + 1), place(2 * it + 2)
        scores(*there, w1)
        pull(*here, w0)
        scores(*after, w0)
        pull(*there, w1)

    scores(0, 3, w1)

    squares = jnp.sum(wide * wide, axis=1, keepdims=True)
    self_weight = jnp.exp(4.0 * squares - 4.0)
    local = jnp.sum(ssum[...]) * SHIFT - jnp.sum(self_weight)
    sums[0] = jnp.full((8, 128), local, F32)
    for c in tell_line:
        c.start()
    pull(0, 2, w0)
    pull(0, 3, w1)
    for c in tell_line:
        c.wait_recv()
    total = sums[0]
    for i in range(len(line)):
        total = total + sums[1 + i]
    sums[16] = total
    for c in tell_plane:
        c.start()

    sum_up[1].wait_recv()
    sum_down[1].wait_recv()
    pulled = (acc[0] + got[0] + got[7]).T * SHIFT - self_weight * wide
    radial = jnp.sum(direction * pulled, axis=1, keepdims=True)
    out_ref[...] = inv_norm * (pulled - direction * radial)
    for c in tell_plane:
        c.wait_recv()
    for i in range(len(plane)):
        total = total + sums[17 + i]
    tot_ref[...] = total
    for c in (first_a + first_b + list(second_a.values()) + list(second_b.values()) + list(sib.values()) + up + down
              + list(sum_up.values()) + list(sum_down.values()) + tell_line + tell_plane):
        c.wait_send()


def per_device(embeddings):
    whole = pl.BlockSpec(memory_space=pltpu.VMEM)
    copies = 6 + 6 + 4 + 8 + 8 + 30
    raw, total = pl.pallas_call(
        kernel,
        out_shape=(jax.ShapeDtypeStruct((B, D), F32), jax.ShapeDtypeStruct((8, 128), F32)),
        in_specs=[whole],
        out_specs=(whole, whole),
        scratch_shapes=[
            pltpu.VMEM((4, 4, 512, D), BF16),
            pltpu.VMEM((4, D, QROWS), BF16),
            pltpu.VMEM((8, D, B), BF16),
            pltpu.VMEM((8, D, B), F32),
            pltpu.VMEM((QROWS, B), BF16),
            pltpu.VMEM((QROWS, B), BF16),
            pltpu.VMEM((8, B), F32),
            pltpu.VMEM((8, D, B), F32),
            pltpu.VMEM((8, D, B), F32),
            pltpu.VMEM((32, 8, 128), F32),
            pltpu.SemaphoreType.DMA((copies,)),
            pltpu.SemaphoreType.DMA((copies,)),
        ],
        compiler_params=pltpu.CompilerParams(
            collective_id=0, has_side_effects=True, vmem_limit_bytes=32 * 2**20),
        name="uniformity",
    )(embeddings)
    pair_total = total[0, 0]
    rows = float(B * lax.axis_size("tour") * lax.axis_size("team"))
    loss = jnp.log(pair_total / (rows * (rows - 1.0)))
    return raw * (rows * rows / 8.0 / pair_total), loss


def solution(mesh):
    return jax.shard_map(
        per_device,
        mesh=mesh,
        in_specs=(P(("tour", "team"), None),),
        out_specs=(P(("tour", "team"), None), P()),
        check_vma=False,
    )
```

```python
import math

import jax
import jax.numpy as jnp
from jax import lax
from jax.experimental import pallas as pl
from jax.experimental.pallas import tpu as pltpu
from jax.sharding import PartitionSpec as P

F32, BF16 = jnp.float32, jnp.bfloat16
MESH = pl.DeviceIdType.MESH
SCALE = 4.0 / math.log(2.0)
SHIFT = math.exp(-4.0)
NX, NY, NZ = 4, 4, 8
D, B = 128, 256
H = B // 2
SPAN = 200.0
MSG = D + 16
LO, HI = pl.ds(0, H), pl.ds(H, H)

OFFSETS = (0, 1, 2, 3, 4, -1, -2, -3)
SLOT = {o: p for p, o in enumerate(OFFSETS)}
CHIPS = ((0, 0), (1, 0), (3, 0), (0, 1), (0, 3), (2, 0), (0, 2), (1, 1), (1, 3), (3, 1), (3, 3),
         (1, 2), (3, 2), (2, 1), (2, 3), (2, 2))
PLACE = {chip: k for k, chip in enumerate(CHIPS)}
GROUPS = ((0, 0, 5), (1, 0, 5), (0, 5, 7), (1, 5, 7), (0, 7, 11), (1, 7, 11), (0, 11, 16), (1, 11, 16))
GROUP_AT = (3.1, 4.4, 4.9, 6.0, 6.3, 7.4, 8.8, 9.9)
ROW_AT = {0: 0.0, 1: 3.0, -1: 3.0, 2: 6.1, -2: 6.1, 3: 9.2, -3: 9.2, 4: 10.2}
SCORE_US, PULL_US = 0.037, 0.018


def plan():
    events = [("rows1", 3.0), ("cols1", 3.1), ("sib1", 4.4), ("cols2", 4.9), ("rows2", 6.0), ("sib2", 6.0),
              ("cols3", 6.3), ("sib3", 7.4), ("cols4", 8.8), ("rows3", 9.2), ("sib4", 9.9), ("rows4", 10.2)]
    n = len(GROUPS)
    goals = [("S", o, g) for g in range(n) for o in (0, 1, 2, 3, 4)]
    goals += [("P", 4, g) for g in range(n)]
    for o in (3, 2, 1):
        goals += [("S", -o, g) for g in range(n)]
        goals += [("P", s * o, g) for s in (-1, 1) for g in range(n)]
    goals += [("P", 0, g) for g in range(n)]
    out, done, now = [], set(), 0.0
    todo = list(goals)

    def finish(kind, offsets):
        return all((kind, o, g) in done for o in offsets for g in range(n))

    after = [("total", lambda: finish("S", (0, 1, 2, 3, 4)))]
    after += [("send4", lambda: finish("P", (4,)))]
    after += [("send3", lambda: finish("P", (3,))), ("send-3", lambda: finish("P", (-3,)))]
    after += [("send1", lambda: finish("P", (1,))), ("send-1", lambda: finish("P", (-1,)))]
    ready2 = lambda o: finish("P", (o,)) and now >= sent.get("send3", 1e9) + 3.8
    after += [("send2", lambda: ready2(2)), ("send-2", lambda: ready2(-2))]
    sent = {}
    while todo or events or after:
        while events and events[0][1] <= now:
            out.append((events.pop(0)[0],))
        for item in list(after):
            if item[1]():
                out.append((item[0],))
                sent[item[0]] = now
                after.remove(item)
                if item[0] == "total":
                    events.append(("plane", now + 5.5))
        pick = None
        for task in todo:
            kind, o, g = task
            if kind == "S":
                if max(GROUP_AT[g], ROW_AT[o]) <= now:
                    pick = task
                    break
            elif ("S", o, g) in done:
                pick = task
                break
        if pick is None:
            now += 0.05
            continue
        todo.remove(pick)
        done.add(pick)
        out.append(pick)
        core, a, b = GROUPS[pick[2]]
        now += (b - a) * (SCORE_US if pick[0] == "S" else PULL_US)
    return out


def dot(a, b):
    return lax.dot_general(a, b, (((1,), (0,)), ((), ())), preferred_element_type=F32)


def encode(x, msg, cols):
    top = (jnp.max(jnp.abs(x), axis=0, keepdims=True) * 1.01 + 1e-30).astype(BF16)
    y = jnp.exp2(jnp.abs(x) * (SPAN / top.astype(F32)) - SPAN / 2)
    msg[0:D, cols] = jnp.where(x < 0, -y, y).astype(BF16)
    msg[D:MSG, cols] = jnp.broadcast_to(top, (MSG - D, x.shape[1]))


def decode(msg, cols):
    y = msg[0:D, cols].astype(F32)
    top = msg[D:MSG, cols].astype(F32)[0:1]
    x = (jnp.log(jnp.abs(y)) * (1.0 / math.log(2.0)) + SPAN / 2) * (top * (1.0 / SPAN))
    return jnp.where(y < 0, -x, x)


class Net:
    def __init__(self, send, recv):
        t, m = lax.axis_index("tour"), lax.axis_index("team")
        self.z = (t // 4) * 2 + (m // 2) % 2
        self.x, self.y, self.c = t % 4, m // 4, m % 2
        self.send, self.recv = send, recv
        self.copies = []

    def at(self, dx=0, dy=0, dz=0, dc=0):
        x, y = (self.x + dx) % NX, (self.y + dy) % NY
        z, c = (self.z + dz) % NZ, (self.c + dc) % 2
        return ((z // 2) * 4 + x, (y * 2 + z % 2) * 2 + c)

    def copy(self, src, dst, **where):
        i = len(self.copies)
        self.copies.append(pltpu.make_async_remote_copy(
            src_ref=src, dst_ref=dst, send_sem=self.send.at[i], recv_sem=self.recv.at[i],
            device_id=self.at(**where), device_id_type=MESH))
        return self.copies[-1]


COPIES = 8 + 6 + 18 + 5 + 8 + 30


def kernel(emb_ref, out_ref, tot_ref, cols, colt, rowt, acc, w, once, twice, mo, mi, sums, send, recv):
    net = Net(send, recv)
    line = [(dz, dc) for dz in range(NZ) for dc in range(2) if (dz, dc) != (0, 0)]
    plane = [(dx, dy) for dx in range(NX) for dy in range(NY) if (dx, dy) != (0, 0)]

    barrier = pltpu.get_barrier_semaphore()
    for dz, dc in line:
        pl.semaphore_signal(barrier, inc=1, device_id=net.at(dz=dz, dc=dc), device_id_type=MESH)
    for dx, dy in plane:
        pl.semaphore_signal(barrier, inc=1, device_id=net.at(dx=dx, dy=dy), device_id_type=MESH)

    row = lambda o: rowt.at[SLOT[o]]
    rows1 = [net.copy(row(0), row(-1), dz=1), net.copy(row(0), row(1), dz=-1)]
    rows2 = [net.copy(row(-1), row(-2), dz=1), net.copy(row(1), row(2), dz=-1)]
    rows3 = [net.copy(row(-2), row(-3), dz=1), net.copy(row(2), row(3), dz=-1)]
    rows4 = [net.copy(rowt.at[SLOT[-2], :, LO], rowt.at[SLOT[4], :, LO], dz=2),
             net.copy(rowt.at[SLOT[2], :, HI], rowt.at[SLOT[4], :, HI], dz=-2)]
    place = lambda dx, dy: PLACE[dx % NX, dy % NY]
    direct = {(dx, dy): net.copy(cols.at[0, 0], cols.at[0, place(-dx, -dy)], dx=dx, dy=dy)
              for dx, dy in ((1, 0), (3, 0), (0, 1), (0, 3), (2, 0), (0, 2))}
    by_y = {(a, b): net.copy(cols.at[0, place(a, 0), LO], cols.at[0, place(a, -b), LO], dy=b)
            for b in (1, 3, 2) for a in (1, 3, 2)}
    by_x = {(a, b): net.copy(cols.at[0, place(0, a), HI], cols.at[0, place(-b, a), HI], dx=b)
            for b in (1, 3, 2) for a in (1, 3, 2)}
    sib = [net.copy(cols.at[0, pl.ds(a, b - a)], cols.at[1, pl.ds(a, b - a)], dc=1)
           for a, b in ((0, 1), (1, 5), (5, 7), (7, 11), (11, 16))]
    far = [net.copy(mo.at[SLOT[4], :, LO], mi.at[0, :, LO], dz=2), net.copy(mo.at[SLOT[4], :, HI], mi.at[1, :, HI], dz=-2)]
    third = {3: net.copy(mo.at[SLOT[3]], mi.at[2], dz=1), -3: net.copy(mo.at[SLOT[-3]], mi.at[3], dz=-1)}
    second = {2: net.copy(mo.at[SLOT[2]], mi.at[4], dz=2), -2: net.copy(mo.at[SLOT[-2]], mi.at[5], dz=-2)}
    first = {1: net.copy(mo.at[SLOT[1]], mi.at[6], dz=1), -1: net.copy(mo.at[SLOT[-1]], mi.at[7], dz=-1)}
    tell_line = [net.copy(sums.at[0], sums.at[1 + i], dz=dz, dc=dc) for i, (dz, dc) in enumerate(line)]
    tell_plane = [net.copy(sums.at[16], sums.at[17 + i], dx=dx, dy=dy) for i, (dx, dy) in enumerate(plane)]

    emb = emb_ref[...]
    inv_norm = lax.rsqrt(jnp.sum(emb * emb, axis=1, keepdims=True) + 1e-06)
    direction = emb * inv_norm
    own = direction.astype(BF16)
    wide = own.astype(F32)
    cols[0, 0] = own
    rowt[0] = wide.T.astype(BF16)
    self_weight = jnp.exp(4.0 * jnp.sum(wide * wide, axis=1, keepdims=True) - 4.0)
    once[...] = jnp.zeros_like(once)
    twice[...] = jnp.zeros_like(twice)
    pl.semaphore_wait(barrier, len(line) + len(plane))

    for c in rows1 + list(direct.values()) + [sib[0]]:
        c.start()

    turned, begun = set(), set()

    def scores(o, g):
        core, a, b = GROUPS[g]
        n = (b - a) * B
        r = (core * 16 + a) * B
        e = jnp.exp2(dot(cols[core, a:b].reshape(n, D), rowt[SLOT[o]]) * SCALE)
        if o >= 0:
            total = once if o in (0, 4) else twice
            total[...] += jnp.sum(e.reshape(n // 64, 64, B), axis=0)
        w[SLOT[o], r:r + n] = e.astype(BF16)

    def pull(o, g):
        core, a, b = GROUPS[g]
        n = (b - a) * B
        r = (core * 16 + a) * B
        if g not in turned:
            turned.add(g)
            for k in range(a, b):
                s = (core * 16 + k) * B
                colt[:, s:s + B] = cols[core, k].astype(F32).T.astype(BF16)
        p = dot(colt[:, r:r + n], w[SLOT[o], r:r + n])
        if o in begun:
            acc[SLOT[o]] += p
        else:
            begun.add(o)
            acc[SLOT[o]] = p

    def wait(copies):
        for c in copies:
            c.wait_recv()

    def start(copies):
        for c in copies:
            c.start()

    near, both = (1, 3), (1, 3, 2)

    def event(name):
        if name == "rows1":
            wait(rows1)
            start(rows2)
        elif name == "rows2":
            wait(rows2)
            start(rows3 + rows4)
        elif name == "rows3":
            wait(rows3)
        elif name == "rows4":
            wait(rows4)
        elif name == "cols1":
            wait([direct[1, 0], direct[3, 0], direct[0, 1], direct[0, 3]])
            start([f[a, b] for b in both for a in near for f in (by_y, by_x)])
            start([sib[1]])
        elif name == "cols2":
            wait([direct[2, 0], direct[0, 2]])
            start([f[2, b] for b in both for f in (by_y, by_x)])
            start([sib[2]])
        elif name == "cols3":
            wait([f[a, b] for b in near for a in near for f in (by_y, by_x)])
            start([sib[3]])
        elif name == "cols4":
            wait([f[a, b] for b in both for a in both for f in (by_y, by_x) if 2 in (a, b)])
            start([sib[4]])
        elif name == "sib1":
            wait(sib[0:2])
        elif name.startswith("sib"):
            wait([sib[int(name[3:])]])
        elif name == "total":
            local = (2.0 * jnp.sum(twice[...]) + jnp.sum(once[...])) * SHIFT - jnp.sum(self_weight)
            sums[0] = jnp.full((8, 128), local, F32)
            start(tell_line)
        elif name == "plane":
            wait(tell_line)
            total = sums[0]
            for i in range(len(line)):
                total = total + sums[1 + i]
            sums[16] = total
            start(tell_plane)
        else:
            o = int(name[4:])
            p = SLOT[o]
            if abs(o) == 2:
                half, i = (LO, 0) if o > 0 else (HI, 1)
                wait([far[i], third[3 if o > 0 else -3]])
                acc[p, :, half] += decode(mi.at[i], half)
                encode(acc[p] + decode(mi.at[2 + i], slice(None)), mo.at[p], slice(None))
                start([second[o]])
            else:
                encode(acc[p], mo.at[p], slice(None))
                start({4: far, 3: [third[3]], -3: [third[-3]], 1: [first[1]], -1: [first[-1]]}[o])

    for task in plan():
        if task[0] == "S":
            scores(*task[1:])
        elif task[0] == "P":
            pull(*task[1:])
        else:
            event(task[0])

    pulled = acc[0]
    for i, c in ((6, first[1]), (7, first[-1]), (4, second[2]), (5, second[-2])):
        c.wait_recv()
        pulled = pulled + decode(mi.at[i], slice(None))
    pulled = pulled.T * SHIFT - self_weight * wide
    radial = jnp.sum(direction * pulled, axis=1, keepdims=True)
    out_ref[...] = inv_norm * (pulled - direction * radial)
    wait(tell_plane)
    total = sums[16]
    for i in range(len(plane)):
        total = total + sums[17 + i]
    tot_ref[...] = total
    for c in net.copies:
        c.wait_send()


def per_device(embeddings):
    whole = pl.BlockSpec(memory_space=pltpu.VMEM)
    raw, total = pl.pallas_call(
        kernel,
        out_shape=(jax.ShapeDtypeStruct((B, D), F32), jax.ShapeDtypeStruct((8, 128), F32)),
        in_specs=[whole],
        out_specs=(whole, whole),
        scratch_shapes=[
            pltpu.VMEM((2, 16, B, D), BF16),
            pltpu.VMEM((D, 32 * B), BF16),
            pltpu.VMEM((8, D, B), BF16),
            pltpu.VMEM((8, D, B), F32),
            pltpu.VMEM((8, 32 * B, B), BF16),
            pltpu.VMEM((64, B), F32),
            pltpu.VMEM((64, B), F32),
            pltpu.VMEM((8, MSG, B), BF16),
            pltpu.VMEM((8, MSG, B), BF16),
            pltpu.VMEM((32, 8, 128), F32),
            pltpu.SemaphoreType.DMA((COPIES,)),
            pltpu.SemaphoreType.DMA((COPIES,)),
        ],
        compiler_params=pltpu.CompilerParams(
            collective_id=0, has_side_effects=True, vmem_limit_bytes=56 * 2**20),
        name="uniformity",
    )(embeddings)
    pair_total = total[0, 0]
    rows = float(B * lax.axis_size("tour") * lax.axis_size("team"))
    loss = jnp.log(pair_total / (rows * (rows - 1.0)))
    return raw * (rows * rows / 8.0 / pair_total), loss


def solution(mesh):
    return jax.shard_map(
        per_device,
        mesh=mesh,
        in_specs=(P(("tour", "team"), None),),
        out_specs=(P(("tour", "team"), None), P()),
        check_vma=False,
    )
```

```python
import math

import jax
import jax.numpy as jnp
from jax import lax
from jax.experimental import pallas as pl
from jax.experimental.pallas import tpu as pltpu
from jax.sharding import PartitionSpec as P

F32, BF16 = jnp.float32, jnp.bfloat16
MESH = pl.DeviceIdType.MESH
SCALE = 4.0 / math.log(2.0)
SHIFT = math.exp(-4.0)
NX, NY, NZ = 4, 4, 8
D, B = 128, 256
H = B // 2
SPAN = 200.0
MSG = D + 16
LO, HI, ALL = pl.ds(0, H), pl.ds(H, H), pl.ds(0, B)

OFFSETS = (0, 1, -1, 2, -2, 3, -3, 4)
SLOT = {o: p for p, o in enumerate(OFFSETS)}
CHIPS = ((0, 0), (1, 0), (3, 0), (0, 1), (0, 3), (2, 0), (0, 2), (1, 1), (1, 3), (3, 1), (3, 3),
         (1, 2), (3, 2), (2, 1), (2, 3), (2, 2))
PLACE = {chip: k for k, chip in enumerate(CHIPS)}
GROUPS = ((0, 0, 5), (1, 0, 5), (0, 5, 7), (1, 5, 7), (0, 7, 11), (1, 7, 11), (0, 11, 15), (1, 11, 15), (0, 15, 16),
          (1, 15, 16))
EVENTS = (("rows1", 3.1), ("cols1", 3.2), ("sib1", 4.9), ("cols2", 5.4), ("sib2", 6.9), ("rows2", 7.5), ("cols3", 7.6),
          ("rows4", 8.4), ("sib3", 9.1), ("cols4", 9.2), ("cols5", 10.2), ("rows3", 10.5), ("sib4", 10.8), ("sib5", 11.7))
AT = dict(EVENTS)
GROUP_AT = tuple(AT[e] for e in ("cols1", "sib1", "cols2", "sib2", "cols3", "sib3", "cols4", "sib4",
                                "cols5", "sib5"))
ROW_AT = {0: 0.0, 1: AT["rows1"], -1: AT["rows1"], 2: AT["rows2"], -2: AT["rows2"], 3: AT["rows3"], -3: AT["rows3"],
          4: AT["rows4"]}
SCORE_US, PULL_US = 0.041, 0.020


def plan():
    events = list(EVENTS)
    n = len(GROUPS)
    goals = [("S", o, g) for g in range(n) for o in (0, 1, 2, 3, 4)]
    goals += [("S", -3, g) for g in range(n)]
    goals += [("P", o, g) for o in (4, 3, -3) for g in range(n)]
    for o in (2, 1):
        goals += [("S", -o, g) for g in range(n)]
        goals += [("P", s * o, g) for s in (-1, 1) for g in range(n)]
    goals += [("P", 0, g) for g in range(n)]
    out, done, now = [], set(), 0.0
    todo = list(goals)

    def finish(kind, offsets):
        return all((kind, o, g) in done for o in offsets for g in range(n))

    after = [("total", lambda: finish("S", (0, 1, 2, 3, 4)))]
    after += [("send4", lambda: finish("P", (4,)))]
    after += [("send3", lambda: finish("P", (3,))), ("send-3", lambda: finish("P", (-3,)))]
    after += [("send1", lambda: finish("P", (1,))), ("send-1", lambda: finish("P", (-1,)))]
    ready2 = lambda o: finish("P", (o,)) and now >= sent.get("send-3", 1e9) + 4.5
    after += [("send2", lambda: ready2(2) and ready2(-2))]
    sent = {}
    while todo or events or after:
        while events and events[0][1] <= now:
            out.append((events.pop(0)[0],))
            now += 0.05
        for item in list(after):
            if item[1]():
                out.append((item[0],))
                sent[item[0]] = now
                after.remove(item)
                if item[0] == "total":
                    events.append(("plane", now + 7.0))
        pick = None
        for task in todo:
            kind, o, g = task
            if kind == "S":
                if max(GROUP_AT[g], ROW_AT[o]) <= now:
                    pick = task
                    break
            elif ("S", o, g) in done:
                pick = task
                break
        if pick is None:
            now += 0.05
            continue
        todo.remove(pick)
        done.add(pick)
        out.append(pick)
        core, a, b = GROUPS[pick[2]]
        now += (b - a) * (SCORE_US if pick[0] == "S" else PULL_US)
    return out


def dot(a, b):
    return lax.dot_general(a, b, (((1,), (0,)), ((), ())), preferred_element_type=F32)


def encode(x, msg, cols):
    top = (jnp.max(jnp.abs(x), axis=0, keepdims=True) * 1.01 + 1e-30).astype(BF16)
    y = jnp.exp2(jnp.abs(x) * (SPAN / top.astype(F32)) - SPAN / 2)
    msg[0:D, cols] = jnp.where(x < 0, -y, y).astype(BF16)
    msg[D:MSG, cols] = jnp.broadcast_to(top, (MSG - D, x.shape[1]))


def decode(msg, cols):
    y = msg[0:D, cols].astype(F32)
    top = msg[D:MSG, cols].astype(F32)[0:1]
    x = (jnp.log(jnp.abs(y)) * (1.0 / math.log(2.0)) + SPAN / 2) * (top * (1.0 / SPAN))
    return jnp.where(y < 0, -x, x)


class Net:
    def __init__(self, send, recv):
        t, m = lax.axis_index("tour"), lax.axis_index("team")
        self.z = (t // 4) * 2 + (m // 2) % 2
        self.x, self.y, self.c = t % 4, m // 4, m % 2
        self.send, self.recv, self.groups, self.known = send, recv, [], {}

    def step(self, axis, d, n):
        if (axis, d) not in self.known:
            v = getattr(self, axis) + d
            v = jnp.where(v >= n, v - n, v) if d else v
            self.known[axis, d] = (v // 2, v % 2) if axis == "z" else v
        return self.known[axis, d]

    def at(self, dx=0, dy=0, dz=0, dc=0):
        z = self.step("z", dz % NZ, NZ)
        return (z[0] * 4 + self.step("x", dx % NX, NX),
                self.step("y", dy % NY, NY) * 4 + z[1] * 2 + self.step("c", dc, 2))


class Group:
    def __init__(self, net, size, *copies):
        i = len(net.groups)
        net.groups.append(self)
        sems = dict(send_sem=net.send.at[i], recv_sem=net.recv.at[i], device_id_type=MESH)
        self.copies = [
            pltpu.make_async_remote_copy(src_ref=a, dst_ref=b, device_id=net.at(**where), **sems) for a, b, where in copies]
        self.all = pltpu.make_async_remote_copy(src_ref=size, dst_ref=size, device_id=net.at(dc=1), **sems)

    def start(self):
        for c in self.copies:
            c.start()

    def wait_recv(self):
        self.all.wait_recv()

    def wait_send(self):
        self.all.wait_send()


NUM_GROUPS = 4 + 5 + 6 + 6 + 2


def kernel(emb_ref, out_ref, tot_ref, cols, colt, rowt, acc, w, once, twice, mo, mi, sums, send, recv):
    net = Net(send, recv)
    line = [(dz, dc) for dz in range(NZ) for dc in range(2) if (dz, dc) != (0, 0)]
    plane = [(dx, dy) for dx in range(NX) for dy in range(NY) if (dx, dy) != (0, 0)]

    barrier = pltpu.get_barrier_semaphore()
    for dz, dc in line:
        pl.semaphore_signal(barrier, inc=1, device_id=net.at(dz=dz, dc=dc), device_id_type=MESH)
    for dx, dy in plane:
        pl.semaphore_signal(barrier, inc=1, device_id=net.at(dx=dx, dy=dy), device_id_type=MESH)

    row = lambda o: rowt.at[SLOT[o]]
    rows1 = Group(net, rowt.at[1:3], (row(0), row(-1), dict(dz=1)), (row(0), row(1), dict(dz=-1)))
    rows2 = Group(net, rowt.at[3:5], (row(-1), row(-2), dict(dz=1)), (row(1), row(2), dict(dz=-1)))
    rows3 = Group(net, rowt.at[5:7], (row(-1), row(-3), dict(dz=2)), (row(1), row(3), dict(dz=-2)))
    rows4 = Group(net, row(4), (row(0), row(4), dict(dz=4)))
    place = lambda dx, dy: PLACE[dx % NX, dy % NY]
    along = lambda dx, dy: (cols.at[0, 0], cols.at[0, place(-dx, -dy)], dict(dx=dx, dy=dy))
    by_y = lambda a, b, s: (cols.at[0, place(a, 0), s], cols.at[0, place(a, -b), s], dict(dy=b))
    by_x = lambda a, b, s: (cols.at[0, place(0, a), s], cols.at[0, place(-b, a), s], dict(dx=b))
    cols1 = Group(net, cols.at[0, 1:5], along(1, 0), along(3, 0), along(0, 1), along(0, 3))
    cols2 = Group(net, cols.at[0, 5:7], along(2, 0), along(0, 2))
    cols3 = Group(net, cols.at[0, 7:11], *[f(a, b, s) for b in (1, 3) for a in (1, 3) for f, s in ((by_y, LO), (by_x, HI))])
    cols4 = Group(net, cols.at[0, 11:15], *[f(a, 2, ALL) for a in (1, 3) for f in (by_y, by_x)])
    cols5 = Group(net, cols.at[0, 15], by_y(2, 2, LO), by_x(2, 2, HI))
    sib = [Group(net, cols.at[1, a:b], (cols.at[0, a:b], cols.at[1, a:b], dict(dc=1)))
           for a, b in ((0, 1), (1, 5), (5, 7), (7, 11), (11, 15), (15, 16))]
    msg = lambda o: mo.at[SLOT[o]]
    far = Group(net, mi.at[0], (msg(4).at[:, LO], mi.at[0, :, LO], dict(dz=2)), (msg(4).at[:, HI], mi.at[0, :, HI], dict(dz=-2)))
    third = {3: Group(net, mi.at[1], (msg(3), mi.at[1], dict(dz=1))), -3: Group(net, mi.at[2], (msg(-3), mi.at[2], dict(dz=-1)))}
    second = Group(net, mi.at[3:5], (msg(2), mi.at[3], dict(dz=2)), (msg(-2), mi.at[4], dict(dz=-2)))
    first = {1: Group(net, mi.at[5], (msg(1), mi.at[5], dict(dz=1))), -1: Group(net, mi.at[6], (msg(-1), mi.at[6], dict(dz=-1)))}
    tell_line = Group(net, sums.at[1:16], *[(sums.at[0], sums.at[1 + i], dict(dz=dz, dc=dc)) for i, (dz, dc) in enumerate(line)])
    tell_plane = Group(
        net, sums.at[17:32], *[(sums.at[16], sums.at[17 + i], dict(dx=dx, dy=dy)) for i, (dx, dy) in enumerate(plane)])

    emb = emb_ref[...]
    inv_norm = lax.rsqrt(jnp.sum(emb * emb, axis=1, keepdims=True) + 1e-06)
    direction = emb * inv_norm
    own = direction.astype(BF16)
    wide = own.astype(F32)
    cols[0, 0] = own
    rowt[0] = wide.T.astype(BF16)
    self_weight = jnp.exp(4.0 * jnp.sum(wide * wide, axis=1, keepdims=True) - 4.0)
    once[...] = jnp.zeros_like(once)
    twice[...] = jnp.zeros_like(twice)
    pl.semaphore_wait(barrier, len(line) + len(plane))

    for c in (rows1, cols1, cols2, rows4, sib[0]):
        c.start()

    turned, begun = set(), set()

    def scores(o, g):
        core, a, b = GROUPS[g]
        n = (b - a) * B
        r = (core * 16 + a) * B
        e = jnp.exp2(dot(cols[core, a:b].reshape(n, D), rowt[SLOT[o]]) * SCALE)
        if o >= 0:
            total = once if o in (0, 4) else twice
            total[...] += jnp.sum(e.reshape(n // 64, 64, B), axis=0)
        w[SLOT[o], r:r + n] = e.astype(BF16)

    def pull(o, g):
        core, a, b = GROUPS[g]
        n = (b - a) * B
        r = (core * 16 + a) * B
        if g not in turned:
            turned.add(g)
            for k in range(a, b):
                s = (core * 16 + k) * B
                colt[:, s:s + B] = cols[core, k].astype(F32).T.astype(BF16)
        p = dot(colt[:, r:r + n], w[SLOT[o], r:r + n])
        if o in begun:
            acc[SLOT[o]] += p
        else:
            begun.add(o)
            acc[SLOT[o]] = p

    def event(name):
        if name == "rows1":
            rows1.wait_recv()
            rows2.start()
            rows3.start()
        elif name.startswith("rows"):
            {"rows2": rows2, "rows3": rows3, "rows4": rows4}[name].wait_recv()
        elif name.startswith("cols"):
            k = int(name[4:])
            (cols1, cols2, cols3, cols4, cols5)[k - 1].wait_recv()
            sib[k].start()
            if k == 1:
                cols3.start()
                cols4.start()
            if k == 2:
                cols5.start()
        elif name.startswith("sib"):
            sib[int(name[3:])].wait_recv()
            if name == "sib1":
                sib[0].wait_recv()
        elif name == "total":
            local = (2.0 * jnp.sum(twice[...]) + jnp.sum(once[...])) * SHIFT - jnp.sum(self_weight)
            sums[0] = jnp.full((8, 128), local, F32)
            tell_line.start()
        elif name == "plane":
            tell_line.wait_recv()
            total = sums[0]
            for i in range(len(line)):
                total = total + sums[1 + i]
            sums[16] = total
            tell_plane.start()
        elif name == "send2":
            far.wait_recv()
            for o, half, i in ((2, LO, 1), (-2, HI, 2)):
                third[3 if o > 0 else -3].wait_recv()
                p = SLOT[o]
                acc[p, :, half] += decode(mi.at[0], half)
                encode(acc[p] + decode(mi.at[i], ALL), mo.at[p], ALL)
            second.start()
        else:
            o = int(name[4:])
            encode(acc[SLOT[o]], mo.at[SLOT[o]], ALL)
            {4: far, 3: third[3], -3: third[-3], 1: first[1], -1: first[-1]}[o].start()

    for task in plan():
        if task[0] == "S":
            scores(*task[1:])
        elif task[0] == "P":
            pull(*task[1:])
        else:
            event(task[0])

    pulled = acc[0]
    for c, held in ((first[-1], (6,)), (first[1], (5,)), (second, (3, 4))):
        c.wait_recv()
        for i in held:
            pulled = pulled + decode(mi.at[i], ALL)
    pulled = pulled.T * SHIFT - self_weight * wide
    radial = jnp.sum(direction * pulled, axis=1, keepdims=True)
    out_ref[...] = inv_norm * (pulled - direction * radial)
    tell_plane.wait_recv()
    total = sums[16]
    for i in range(len(plane)):
        total = total + sums[17 + i]
    tot_ref[...] = total
    for c in net.groups:
        c.wait_send()


def per_device(embeddings):
    whole = pl.BlockSpec(memory_space=pltpu.VMEM)
    raw, total = pl.pallas_call(
        kernel,
        out_shape=(jax.ShapeDtypeStruct((B, D), F32), jax.ShapeDtypeStruct((8, 128), F32)),
        in_specs=[whole],
        out_specs=(whole, whole),
        scratch_shapes=[
            pltpu.VMEM((2, 16, B, D), BF16),
            pltpu.VMEM((D, 32 * B), BF16),
            pltpu.VMEM((8, D, B), BF16),
            pltpu.VMEM((8, D, B), F32),
            pltpu.VMEM((8, 32 * B, B), BF16),
            pltpu.VMEM((64, B), F32),
            pltpu.VMEM((64, B), F32),
            pltpu.VMEM((8, MSG, B), BF16),
            pltpu.VMEM((8, MSG, B), BF16),
            pltpu.VMEM((32, 8, 128), F32),
            pltpu.SemaphoreType.DMA((NUM_GROUPS,)),
            pltpu.SemaphoreType.DMA((NUM_GROUPS,)),
        ],
        compiler_params=pltpu.CompilerParams(
            collective_id=0, has_side_effects=True, vmem_limit_bytes=56 * 2**20),
        name="uniformity",
    )(embeddings)
    pair_total = total[0, 0]
    rows = float(B * lax.axis_size("tour") * lax.axis_size("team"))
    loss = jnp.log(pair_total / (rows * (rows - 1.0)))
    return raw * (rows * rows / 8.0 / pair_total), loss


def solution(mesh):
    return jax.shard_map(
        per_device,
        mesh=mesh,
        in_specs=(P(("tour", "team"), None),),
        out_specs=(P(("tour", "team"), None), P()),
        check_vma=False,
    )
```

```python
import math

import jax
import jax.numpy as jnp
from jax import lax
from jax.experimental import pallas as pl
from jax.experimental.pallas import tpu as pltpu
from jax.sharding import PartitionSpec as P

F32, BF16 = jnp.float32, jnp.bfloat16
MESH = pl.DeviceIdType.MESH
SCALE = 4.0 / math.log(2.0)
SHIFT = math.exp(-4.0)
NX, NY, NZ = 4, 4, 8
D, B = 128, 256
H = B // 2
SPAN = 200.0
MSG = D + 16
LO, HI, ALL = pl.ds(0, H), pl.ds(H, H), pl.ds(0, B)

OFFSETS = (0, 1, -1, 2, -2, 3, -3, 4)
SLOT = {o: p for p, o in enumerate(OFFSETS)}
CHIPS = ((0, 0), (1, 0), (3, 0), (0, 1), (0, 3), (2, 0), (0, 2), (1, 1), (1, 3), (3, 1), (3, 3),
         (1, 2), (3, 2), (2, 1), (2, 3), (2, 2))
PLACE = {chip: k for k, chip in enumerate(CHIPS)}
GROUPS = ((0, 0, 5), (1, 0, 5), (0, 5, 7), (1, 5, 7), (0, 7, 11), (1, 7, 11), (0, 11, 15), (1, 11, 15), (0, 15, 16),
          (1, 15, 16))
EVENTS = (("rows1", 3.1), ("cols1", 3.1), ("cols2", 5.2), ("sib1", 5.2), ("rows2", 7.4), ("cols3", 7.4), ("sib2", 7.4),
          ("rows4", 8.9), ("sib3", 8.9), ("cols4", 10.0), ("cols5", 10.0), ("rows3", 10.4), ("sib4", 11.5), ("sib5", 11.5))
AT = dict(EVENTS)
GROUP_AT = tuple(AT[e] for e in ("cols1", "sib1", "cols2", "sib2", "cols3", "sib3", "cols4", "sib4",
                                "cols5", "sib5"))
ROW_AT = {0: 0.0, 1: AT["rows1"], -1: AT["rows1"], 2: AT["rows2"], -2: AT["rows2"], 3: AT["rows3"], -3: AT["rows3"],
          4: AT["rows4"]}
SCORE_US, PULL_US = 0.041, 0.020


def plan():
    events = list(EVENTS)
    n = len(GROUPS)
    goals = [(kind, o, g) for o in (4, 3, -3) for kind in "SP" for g in range(n)]
    goals += [("S", o, g) for g in range(n) for o in (0, 1, 2)]
    for o in (2, 1):
        goals += [("S", -o, g) for g in range(n)]
        goals += [("P", s * o, g) for s in (-1, 1) for g in range(n)]
    goals += [("P", 0, g) for g in range(n)]
    out, done, now = [], set(), 0.0
    todo = list(goals)

    def finish(kind, offsets):
        return all((kind, o, g) in done for o in offsets for g in range(n))

    after = [("total", lambda: finish("S", (0, 1, 2, 3, 4)))]
    after += [("send4", lambda: finish("P", (4,)))]
    after += [("send3", lambda: finish("P", (3,))), ("send-3", lambda: finish("P", (-3,)))]
    after += [("send1", lambda: finish("P", (1,))), ("send-1", lambda: finish("P", (-1,)))]
    ready2 = lambda o: finish("P", (o,)) and now >= sent.get("send-3", 1e9) + 4.2
    after += [("send2", lambda: ready2(2) and ready2(-2))]
    sent = {}
    while todo or events or after:
        while events and events[0][1] <= now:
            out.append((events.pop(0)[0],))
            now += 0.05
        for item in list(after):
            if item[1]():
                out.append((item[0],))
                sent[item[0]] = now
                after.remove(item)
                if item[0] == "total":
                    events.append(("plane", now + 5.5))
        pick = None
        for task in todo:
            kind, o, g = task
            if kind == "S":
                if max(GROUP_AT[g], ROW_AT[o]) <= now:
                    pick = task
                    break
            elif ("S", o, g) in done:
                pick = task
                break
        if pick is None:
            now += 0.05
            continue
        todo.remove(pick)
        done.add(pick)
        out.append(pick)
        core, a, b = GROUPS[pick[2]]
        now += (b - a) * (SCORE_US if pick[0] == "S" else PULL_US)
    return out


def dot(a, b):
    return lax.dot_general(a, b, (((1,), (0,)), ((), ())), preferred_element_type=F32)


def encode(x, msg, cols):
    top = (jnp.max(jnp.abs(x), axis=0, keepdims=True) * 1.01 + 1e-30).astype(BF16)
    y = jnp.exp2(jnp.abs(x) * (SPAN / top.astype(F32)) - SPAN / 2)
    msg[0:D, cols] = jnp.where(x < 0, -y, y).astype(BF16)
    msg[D:MSG, cols] = jnp.broadcast_to(top, (MSG - D, x.shape[1]))


def decode(msg, cols):
    y = msg[0:D, cols].astype(F32)
    top = msg[D:MSG, cols].astype(F32)[0:1]
    x = (jnp.log(jnp.abs(y)) * (1.0 / math.log(2.0)) + SPAN / 2) * (top * (1.0 / SPAN))
    return jnp.where(y < 0, -x, x)


class Net:
    def __init__(self, send, recv):
        t, m = lax.axis_index("tour"), lax.axis_index("team")
        self.z = (t // 4) * 2 + (m // 2) % 2
        self.x, self.y, self.c = t % 4, m // 4, m % 2
        self.send, self.recv, self.groups, self.known = send, recv, [], {}

    def step(self, axis, d, n):
        if (axis, d) not in self.known:
            v = getattr(self, axis) + d
            v = jnp.where(v >= n, v - n, v) if d else v
            self.known[axis, d] = (v // 2, v % 2) if axis == "z" else v
        return self.known[axis, d]

    def at(self, dx=0, dy=0, dz=0, dc=0):
        z = self.step("z", dz % NZ, NZ)
        return (z[0] * 4 + self.step("x", dx % NX, NX),
                self.step("y", dy % NY, NY) * 4 + z[1] * 2 + self.step("c", dc, 2))


class Group:
    def __init__(self, net, size, *copies):
        i = len(net.groups)
        net.groups.append(self)
        sems = dict(send_sem=net.send.at[i], recv_sem=net.recv.at[i], device_id_type=MESH)
        self.copies = [
            pltpu.make_async_remote_copy(src_ref=a, dst_ref=b, device_id=net.at(**where), **sems) for a, b, where in copies]
        self.all = pltpu.make_async_remote_copy(src_ref=size, dst_ref=size, device_id=net.at(dc=1), **sems)

    def start(self):
        for c in self.copies:
            c.start()

    def wait_recv(self):
        self.all.wait_recv()

    def wait_send(self):
        self.all.wait_send()


NUM_GROUPS = 4 + 5 + 6 + 6 + 2


def kernel(emb_hbm, out_ref, loss_ref, emb_ref, fetched, cols, colt, rowt, acc, w, once, twice, mo, mi, sums, send, recv):
    net = Net(send, recv)
    line = [(dz, dc) for dz in range(NZ) for dc in range(2) if (dz, dc) != (0, 0)]
    plane = [(dx, dy) for dx in range(NX) for dy in range(NY) if (dx, dy) != (0, 0)]

    barrier = pltpu.get_barrier_semaphore()
    for dz, dc in line:
        pl.semaphore_signal(barrier, inc=1, device_id=net.at(dz=dz, dc=dc), device_id_type=MESH)
    for dx, dy in plane:
        pl.semaphore_signal(barrier, inc=1, device_id=net.at(dx=dx, dy=dy), device_id_type=MESH)

    fetch = pltpu.make_async_copy(emb_hbm, emb_ref, fetched)
    fetch.start()

    row = lambda o: rowt.at[SLOT[o]]
    rows1 = Group(net, rowt.at[1:3], (row(0), row(-1), dict(dz=1)), (row(0), row(1), dict(dz=-1)))
    rows2 = Group(net, rowt.at[3:5], (row(-1), row(-2), dict(dz=1)), (row(1), row(2), dict(dz=-1)))
    rows3 = Group(net, rowt.at[5:7], (row(-1), row(-3), dict(dz=2)), (row(1), row(3), dict(dz=-2)))
    rows4 = Group(net, row(4), (row(0), row(4), dict(dz=4)))
    place = lambda dx, dy: PLACE[dx % NX, dy % NY]
    along = lambda dx, dy: (cols.at[0, 0], cols.at[0, place(-dx, -dy)], dict(dx=dx, dy=dy))
    by_y = lambda a, b, s: (cols.at[0, place(a, 0), s], cols.at[0, place(a, -b), s], dict(dy=b))
    by_x = lambda a, b, s: (cols.at[0, place(0, a), s], cols.at[0, place(-b, a), s], dict(dx=b))
    cols1 = Group(net, cols.at[0, 1:5], along(1, 0), along(3, 0), along(0, 1), along(0, 3))
    cols2 = Group(net, cols.at[0, 5:7], along(2, 0), along(0, 2))
    cols3 = Group(net, cols.at[0, 7:11], *[f(a, b, s) for b in (1, 3) for a in (1, 3) for f, s in ((by_y, LO), (by_x, HI))])
    cols4 = Group(net, cols.at[0, 11:15], *[f(a, 2, ALL) for a in (1, 3) for f in (by_y, by_x)])
    cols5 = Group(net, cols.at[0, 15], by_y(2, 2, LO), by_x(2, 2, HI))
    sib = [Group(net, cols.at[1, a:b], (cols.at[0, a:b], cols.at[1, a:b], dict(dc=1)))
           for a, b in ((0, 1), (1, 5), (5, 7), (7, 11), (11, 15), (15, 16))]
    msg = lambda o: mo.at[SLOT[o]]
    far = Group(net, mi.at[0], (msg(4).at[:, LO], mi.at[0, :, LO], dict(dz=2)), (msg(4).at[:, HI], mi.at[0, :, HI], dict(dz=-2)))
    third = {3: Group(net, mi.at[1], (msg(3), mi.at[1], dict(dz=1))), -3: Group(net, mi.at[2], (msg(-3), mi.at[2], dict(dz=-1)))}
    second = Group(net, mi.at[3:5], (msg(2), mi.at[3], dict(dz=2)), (msg(-2), mi.at[4], dict(dz=-2)))
    first = {1: Group(net, mi.at[5], (msg(1), mi.at[5], dict(dz=1))), -1: Group(net, mi.at[6], (msg(-1), mi.at[6], dict(dz=-1)))}
    tell_line = Group(net, sums.at[1:16], *[(sums.at[0], sums.at[1 + i], dict(dz=dz, dc=dc)) for i, (dz, dc) in enumerate(line)])
    tell_plane = Group(
        net, sums.at[17:32], *[(sums.at[16], sums.at[17 + i], dict(dx=dx, dy=dy)) for i, (dx, dy) in enumerate(plane)])

    fetch.wait()
    emb = emb_ref[...]
    inv_norm = lax.rsqrt(jnp.sum(emb * emb, axis=1, keepdims=True) + 1e-06)
    direction = emb * inv_norm
    own = direction.astype(BF16)
    wide = own.astype(F32)
    cols[0, 0] = own
    rowt[0] = wide.T.astype(BF16)
    self_weight = jnp.exp(4.0 * jnp.sum(wide * wide, axis=1, keepdims=True) - 4.0)
    once[...] = jnp.zeros_like(once)
    twice[...] = jnp.zeros_like(twice)
    pl.semaphore_wait(barrier, len(line) + len(plane))

    for c in (rows1, cols1, cols2, rows4, sib[0]):
        c.start()

    turned, begun = set(), set()

    def scores(o, g):
        core, a, b = GROUPS[g]
        n = (b - a) * B
        r = (core * 16 + a) * B
        e = jnp.exp2(dot(cols[core, a:b].reshape(n, D), rowt[SLOT[o]]) * SCALE)
        if o >= 0:
            total = once if o in (0, 4) else twice
            total[...] += jnp.sum(e.reshape(n // 64, 64, B), axis=0)
        w[SLOT[o], r:r + n] = e.astype(BF16)

    def pull(o, g):
        core, a, b = GROUPS[g]
        n = (b - a) * B
        r = (core * 16 + a) * B
        if g not in turned:
            turned.add(g)
            for k in range(a, b):
                s = (core * 16 + k) * B
                colt[:, s:s + B] = cols[core, k].astype(F32).T.astype(BF16)
        p = dot(colt[:, r:r + n], w[SLOT[o], r:r + n])
        if o in begun:
            acc[SLOT[o]] += p
        else:
            begun.add(o)
            acc[SLOT[o]] = p

    def event(name):
        if name == "rows1":
            rows1.wait_recv()
            rows2.start()
            rows3.start()
        elif name.startswith("rows"):
            {"rows2": rows2, "rows3": rows3, "rows4": rows4}[name].wait_recv()
        elif name.startswith("cols"):
            k = int(name[4:])
            (cols1, cols2, cols3, cols4, cols5)[k - 1].wait_recv()
            sib[k].start()
            if k == 1:
                cols3.start()
                cols4.start()
            if k == 2:
                cols5.start()
        elif name.startswith("sib"):
            sib[int(name[3:])].wait_recv()
            if name == "sib1":
                sib[0].wait_recv()
        elif name == "total":
            local = (2.0 * jnp.sum(twice[...]) + jnp.sum(once[...])) * SHIFT - jnp.sum(self_weight)
            sums[0] = jnp.full((8, 128), local, F32)
            tell_line.start()
        elif name == "plane":
            tell_line.wait_recv()
            total = sums[0]
            for i in range(len(line)):
                total = total + sums[1 + i]
            sums[16] = total
            tell_plane.start()
        elif name == "send2":
            far.wait_recv()
            for o, half, i in ((2, LO, 1), (-2, HI, 2)):
                third[3 if o > 0 else -3].wait_recv()
                p = SLOT[o]
                acc[p, :, half] += decode(mi.at[0], half)
                encode(acc[p] + decode(mi.at[i], ALL), mo.at[p], ALL)
            second.start()
        else:
            o = int(name[4:])
            encode(acc[SLOT[o]], mo.at[SLOT[o]], ALL)
            {4: far, 3: third[3], -3: third[-3], 1: first[1], -1: first[-1]}[o].start()

    for task in plan():
        if task[0] == "S":
            scores(*task[1:])
        elif task[0] == "P":
            pull(*task[1:])
        else:
            event(task[0])

    pulled = acc[0]
    for c, held in ((first[-1], (6,)), (first[1], (5,)), (second, (3, 4))):
        c.wait_recv()
        for i in held:
            pulled = pulled + decode(mi.at[i], ALL)
    pulled = pulled.T * SHIFT - self_weight * wide
    radial = jnp.sum(direction * pulled, axis=1, keepdims=True)
    grad = inv_norm * (pulled - direction * radial)
    tell_plane.wait_recv()
    total = sums[16]
    for i in range(len(plane)):
        total = total + sums[17 + i]
    rows = float(B * lax.axis_size("tour") * lax.axis_size("team"))
    out_ref[...] = grad * jnp.broadcast_to((rows * rows / 8.0) / total[0:1], (B, D))
    loss_ref[0, 0] = jnp.max(jnp.log(total / (rows * (rows - 1.0))))
    for c in net.groups:
        c.wait_send()


def per_device(embeddings):
    whole = pl.BlockSpec(memory_space=pltpu.VMEM)
    grad, loss = pl.pallas_call(
        kernel,
        out_shape=(jax.ShapeDtypeStruct((B, D), F32), jax.ShapeDtypeStruct((1, 1), F32)),
        in_specs=[pl.BlockSpec(memory_space=pltpu.HBM)],
        out_specs=(whole, pl.BlockSpec(memory_space=pltpu.SMEM)),
        scratch_shapes=[
            pltpu.VMEM((B, D), F32),
            pltpu.SemaphoreType.DMA,
            pltpu.VMEM((2, 16, B, D), BF16),
            pltpu.VMEM((D, 32 * B), BF16),
            pltpu.VMEM((8, D, B), BF16),
            pltpu.VMEM((8, D, B), F32),
            pltpu.VMEM((8, 32 * B, B), BF16),
            pltpu.VMEM((64, B), F32),
            pltpu.VMEM((64, B), F32),
            pltpu.VMEM((8, MSG, B), BF16),
            pltpu.VMEM((8, MSG, B), BF16),
            pltpu.VMEM((32, 8, 128), F32),
            pltpu.SemaphoreType.DMA((NUM_GROUPS,)),
            pltpu.SemaphoreType.DMA((NUM_GROUPS,)),
        ],
        compiler_params=pltpu.CompilerParams(
            collective_id=0, has_side_effects=True, vmem_limit_bytes=56 * 2**20),
        name="uniformity",
    )(embeddings)
    return grad, loss.reshape(())


def solution(mesh):
    return jax.shard_map(
        per_device,
        mesh=mesh,
        in_specs=(P(("tour", "team"), None),),
        out_specs=(P(("tour", "team"), None), P()),
        check_vma=False,
    )
```

```python
import math

import jax
import jax.numpy as jnp
from jax import lax
from jax.experimental import pallas as pl
from jax.experimental.pallas import tpu as pltpu
from jax.sharding import PartitionSpec as P

F32, BF16 = jnp.float32, jnp.bfloat16
MESH = pl.DeviceIdType.MESH
SCALE = 4.0 / math.log(2.0)
SHIFT = math.exp(-4.0)
NX, NY, NZ = 4, 4, 8
D, B = 128, 256
H = B // 2
SPAN = 200.0
MSG = D + 16
LO, HI, ALL = pl.ds(0, H), pl.ds(H, H), pl.ds(0, B)

OFFSETS = (0, 1, -1, 2, -2, 3, -3, 4)
SLOT = {o: p for p, o in enumerate(OFFSETS)}
CHIPS = ((0, 0), (1, 0), (3, 0), (0, 1), (0, 3), (2, 0), (0, 2), (1, 1), (1, 3), (3, 1), (3, 3),
         (1, 2), (3, 2), (2, 1), (2, 3), (2, 2))
PLACE = {chip: k for k, chip in enumerate(CHIPS)}
GROUPS = ((0, 0, 5), (1, 0, 5), (0, 5, 7), (1, 5, 7), (0, 7, 11), (1, 7, 11), (0, 11, 15), (1, 11, 15), (0, 15, 16),
          (1, 15, 16))
EVENTS = (("rows1", 3.1), ("cols1", 3.1), ("cols2", 5.2), ("sib1", 5.2), ("rows2", 7.4), ("cols3", 7.4), ("sib2", 7.4),
          ("rows4", 8.9), ("sib3", 8.9), ("cols4", 10.0), ("cols5", 10.0), ("rows3", 10.4), ("sib4", 11.5), ("sib5", 11.5))
AT = dict(EVENTS)
GROUP_AT = tuple(AT[e] for e in ("cols1", "sib1", "cols2", "sib2", "cols3", "sib3", "cols4", "sib4",
                                "cols5", "sib5"))
ROW_AT = {0: 0.0, 1: AT["rows1"], -1: AT["rows1"], 2: AT["rows2"], -2: AT["rows2"], 3: AT["rows3"], -3: AT["rows3"],
          4: AT["rows4"]}
SCORE_US, PULL_US = 0.041, 0.020


def plan():
    events = list(EVENTS)
    n = len(GROUPS)
    goals = [(kind, o, g) for o in (4, 3, -3) for kind in "SP" for g in range(n)]
    goals += [("S", o, g) for g in range(n) for o in (0, 1, 2)]
    for o in (2, 1):
        goals += [("S", -o, g) for g in range(n)]
        goals += [("P", s * o, g) for s in (-1, 1) for g in range(n)]
    goals += [("P", 0, g) for g in range(n)]
    out, done, now = [], set(), 0.0
    todo = list(goals)

    def finish(kind, offsets):
        return all((kind, o, g) in done for o in offsets for g in range(n))

    after = [("total", lambda: finish("S", (0, 1, 2, 3, 4)))]
    after += [("send4", lambda: finish("P", (4,)))]
    after += [("send3", lambda: finish("P", (3,))), ("send-3", lambda: finish("P", (-3,)))]
    after += [("send1", lambda: finish("P", (1,))), ("send-1", lambda: finish("P", (-1,)))]
    ready2 = lambda o: finish("P", (o,)) and now >= sent.get("send-3", 1e9) + 4.2
    after += [("send2", lambda: ready2(2) and ready2(-2))]
    sent = {}
    while todo or events or after:
        while events and events[0][1] <= now:
            out.append((events.pop(0)[0],))
            now += 0.05
        for item in list(after):
            if item[1]():
                out.append((item[0],))
                sent[item[0]] = now
                after.remove(item)
                if item[0] == "total":
                    events += [("told1", now + 4.2), ("told2", now + 7.4)]
        pick = None
        for task in todo:
            kind, o, g = task
            if kind == "S":
                if max(GROUP_AT[g], ROW_AT[o]) <= now:
                    pick = task
                    break
            elif ("S", o, g) in done:
                pick = task
                break
        if pick is None:
            now += 0.05
            continue
        todo.remove(pick)
        done.add(pick)
        out.append(pick)
        core, a, b = GROUPS[pick[2]]
        now += (b - a) * (SCORE_US if pick[0] == "S" else PULL_US)
    return out


def dot(a, b):
    return lax.dot_general(a, b, (((1,), (0,)), ((), ())), preferred_element_type=F32)


def encode(x, msg, cols):
    top = (jnp.max(jnp.abs(x), axis=0, keepdims=True) * 1.01 + 1e-30).astype(BF16)
    y = jnp.exp2(jnp.abs(x) * (SPAN / top.astype(F32)) - SPAN / 2)
    msg[0:D, cols] = jnp.where(x < 0, -y, y).astype(BF16)
    msg[D:MSG, cols] = jnp.broadcast_to(top, (MSG - D, x.shape[1]))


def decode(msg, cols):
    y = msg[0:D, cols].astype(F32)
    top = msg[D:MSG, cols].astype(F32)[0:1]
    x = (jnp.log(jnp.abs(y)) * (1.0 / math.log(2.0)) + SPAN / 2) * (top * (1.0 / SPAN))
    return jnp.where(y < 0, -x, x)


class Net:
    def __init__(self, send, recv):
        t, m = lax.axis_index("tour"), lax.axis_index("team")
        self.z = (t // 4) * 2 + (m // 2) % 2
        self.x, self.y, self.c = t % 4, m // 4, m % 2
        self.send, self.recv, self.groups, self.known = send, recv, [], {}

    def step(self, axis, d, n):
        if (axis, d) not in self.known:
            v = getattr(self, axis) + d
            v = jnp.where(v >= n, v - n, v) if d else v
            self.known[axis, d] = (v // 2, v % 2) if axis == "z" else v
        return self.known[axis, d]

    def at(self, dx=0, dy=0, dz=0, dc=0):
        z = self.step("z", dz % NZ, NZ)
        return (z[0] * 4 + self.step("x", dx % NX, NX),
                self.step("y", dy % NY, NY) * 4 + z[1] * 2 + self.step("c", dc, 2))


class Group:
    def __init__(self, net, size, *copies):
        i = len(net.groups)
        net.groups.append(self)
        sems = dict(send_sem=net.send.at[i], recv_sem=net.recv.at[i], device_id_type=MESH)
        self.copies = [
            pltpu.make_async_remote_copy(src_ref=a, dst_ref=b, device_id=net.at(**where), **sems) for a, b, where in copies]
        self.all = pltpu.make_async_remote_copy(src_ref=size, dst_ref=size, device_id=net.at(dc=1), **sems)

    def start(self):
        for c in self.copies:
            c.start()

    def wait_recv(self):
        self.all.wait_recv()

    def wait_send(self):
        self.all.wait_send()


NUM_GROUPS = 4 + 5 + 6 + 6 + 3


def kernel(emb_hbm, out_ref, loss_ref, factor_ref, emb_ref, fetched, cols, colt, rowt, acc, w, once, twice, mo, mi, sums, send, recv):
    net = Net(send, recv)
    along_z = [dict(dz=d) for d in range(1, NZ)]
    along_x = [dict(dx=d, dc=c) for d in range(NX) for c in range(2) if (d, c) != (0, 0)]
    along_y = [dict(dy=d) for d in range(1, NY)]
    met = along_z + along_x + along_y

    barrier = pltpu.get_barrier_semaphore()
    for where in met:
        pl.semaphore_signal(barrier, inc=1, device_id=net.at(**where), device_id_type=MESH)
    fetch = pltpu.make_async_copy(emb_hbm, emb_ref, fetched)
    fetch.start()

    row = lambda o: rowt.at[SLOT[o]]
    rows1 = Group(net, rowt.at[1:3], (row(0), row(-1), dict(dz=1)), (row(0), row(1), dict(dz=-1)))
    rows2 = Group(net, rowt.at[3:5], (row(-1), row(-2), dict(dz=1)), (row(1), row(2), dict(dz=-1)))
    rows3 = Group(net, rowt.at[5:7], (row(-1), row(-3), dict(dz=2)), (row(1), row(3), dict(dz=-2)))
    rows4 = Group(net, row(4), (row(0), row(4), dict(dz=4)))
    place = lambda dx, dy: PLACE[dx % NX, dy % NY]
    along = lambda dx, dy: (cols.at[0, 0], cols.at[0, place(-dx, -dy)], dict(dx=dx, dy=dy))
    by_y = lambda a, b, s: (cols.at[0, place(a, 0), s], cols.at[0, place(a, -b), s], dict(dy=b))
    by_x = lambda a, b, s: (cols.at[0, place(0, a), s], cols.at[0, place(-b, a), s], dict(dx=b))
    cols1 = Group(net, cols.at[0, 1:5], along(1, 0), along(3, 0), along(0, 1), along(0, 3))
    cols2 = Group(net, cols.at[0, 5:7], along(2, 0), along(0, 2))
    cols3 = Group(net, cols.at[0, 7:11], *[f(a, b, s) for b in (1, 3) for a in (1, 3) for f, s in ((by_y, LO), (by_x, HI))])
    cols4 = Group(net, cols.at[0, 11:15], *[f(a, 2, ALL) for a in (1, 3) for f in (by_y, by_x)])
    cols5 = Group(net, cols.at[0, 15], by_y(2, 2, LO), by_x(2, 2, HI))
    sib = [Group(net, cols.at[1, a:b], (cols.at[0, a:b], cols.at[1, a:b], dict(dc=1)))
           for a, b in ((0, 1), (1, 5), (5, 7), (7, 11), (11, 15), (15, 16))]
    msg = lambda o: mo.at[SLOT[o]]
    far = Group(net, mi.at[0], (msg(4).at[:, LO], mi.at[0, :, LO], dict(dz=2)), (msg(4).at[:, HI], mi.at[0, :, HI], dict(dz=-2)))
    third = {3: Group(net, mi.at[1], (msg(3), mi.at[1], dict(dz=1))), -3: Group(net, mi.at[2], (msg(-3), mi.at[2], dict(dz=-1)))}
    second = Group(net, mi.at[3:5], (msg(2), mi.at[3], dict(dz=2)), (msg(-2), mi.at[4], dict(dz=-2)))
    first = {1: Group(net, mi.at[5], (msg(1), mi.at[5], dict(dz=1))), -1: Group(net, mi.at[6], (msg(-1), mi.at[6], dict(dz=-1)))}
    tell = []
    for base, peers in ((0, along_z), (8, along_x), (16, along_y)):
        tell.append(Group(net, sums.at[base + 1:base + 1 + len(peers)],
                          *[(sums.at[base], sums.at[base + 1 + i], where) for i, where in enumerate(peers)]))

    def told(r):
        tell[r].wait_recv()
        total = sums[8 * r]
        for i in range(len(tell[r].copies)):
            total = total + sums[8 * r + 1 + i]
        return total

    fetch.wait()
    emb = emb_ref[...]
    inv_norm = lax.rsqrt(jnp.sum(emb * emb, axis=1, keepdims=True) + 1e-06)
    direction = emb * inv_norm
    own = direction.astype(BF16)
    wide = own.astype(F32)
    cols[0, 0] = own
    rowt[0] = wide.T.astype(BF16)
    self_weight = jnp.exp(4.0 * jnp.sum(wide * wide, axis=1, keepdims=True) - 4.0)
    once[...] = jnp.zeros_like(once)
    twice[...] = jnp.zeros_like(twice)
    pl.semaphore_wait(barrier, len(met))

    for c in (rows1, cols1, cols2, rows4, sib[0]):
        c.start()

    turned, begun = set(), set()

    def scores(o, g):
        core, a, b = GROUPS[g]
        n = (b - a) * B
        r = (core * 16 + a) * B
        e = jnp.exp2(dot(cols[core, a:b].reshape(n, D), rowt[SLOT[o]]) * SCALE)
        if o >= 0:
            total = once if o in (0, 4) else twice
            total[...] += jnp.sum(e.reshape(n // 64, 64, B), axis=0)
        w[SLOT[o], r:r + n] = e.astype(BF16)

    def pull(o, g):
        core, a, b = GROUPS[g]
        n = (b - a) * B
        r = (core * 16 + a) * B
        if g not in turned:
            turned.add(g)
            for k in range(a, b):
                s = (core * 16 + k) * B
                colt[:, s:s + B] = cols[core, k].astype(F32).T.astype(BF16)
        p = dot(colt[:, r:r + n], w[SLOT[o], r:r + n])
        if o in begun:
            acc[SLOT[o]] += p
        else:
            begun.add(o)
            acc[SLOT[o]] = p

    def event(name):
        if name == "rows1":
            rows1.wait_recv()
            rows2.start()
            rows3.start()
        elif name.startswith("rows"):
            {"rows2": rows2, "rows3": rows3, "rows4": rows4}[name].wait_recv()
        elif name.startswith("cols"):
            k = int(name[4:])
            (cols1, cols2, cols3, cols4, cols5)[k - 1].wait_recv()
            sib[k].start()
            if k == 1:
                cols3.start()
                cols4.start()
            if k == 2:
                cols5.start()
        elif name.startswith("sib"):
            sib[int(name[3:])].wait_recv()
            if name == "sib1":
                sib[0].wait_recv()
        elif name == "total":
            local = (2.0 * jnp.sum(twice[...]) + jnp.sum(once[...])) * SHIFT - jnp.sum(self_weight)
            sums[0] = jnp.full((8, 128), local, F32)
            tell[0].start()
        elif name.startswith("told"):
            r = int(name[4:])
            sums[8 * r] = told(r - 1)
            tell[r].start()
        elif name == "send2":
            far.wait_recv()
            for o, half, i in ((2, LO, 1), (-2, HI, 2)):
                third[3 if o > 0 else -3].wait_recv()
                p = SLOT[o]
                acc[p, :, half] += decode(mi.at[0], half)
                encode(acc[p] + decode(mi.at[i], ALL), mo.at[p], ALL)
            second.start()
        else:
            o = int(name[4:])
            encode(acc[SLOT[o]], mo.at[SLOT[o]], ALL)
            {4: far, 3: third[3], -3: third[-3], 1: first[1], -1: first[-1]}[o].start()

    for task in plan():
        if task[0] == "S":
            scores(*task[1:])
        elif task[0] == "P":
            pull(*task[1:])
        else:
            event(task[0])

    pulled = acc[0]
    for c, held in ((first[-1], (6,)), (first[1], (5,)), (second, (3, 4))):
        c.wait_recv()
        for i in held:
            pulled = pulled + decode(mi.at[i], ALL)
    pulled = pulled.T * SHIFT - self_weight * wide
    radial = jnp.sum(direction * pulled, axis=1, keepdims=True)
    out_ref[...] = inv_norm * (pulled - direction * radial)
    total = told(2)
    rows = float(B * lax.axis_size("tour") * lax.axis_size("team"))
    loss_ref[0, 0] = jnp.max(jnp.log(total / (rows * (rows - 1.0))))
    factor_ref[0, 0] = jnp.max((rows * rows / 8.0) / total)
    for c in net.groups:
        c.wait_send()


def per_device(embeddings):
    whole = pl.BlockSpec(memory_space=pltpu.VMEM)
    grad, loss, factor = pl.pallas_call(
        kernel,
        out_shape=(jax.ShapeDtypeStruct((B, D), F32), jax.ShapeDtypeStruct((1, 1), F32), jax.ShapeDtypeStruct((1, 1), F32)),
        in_specs=[pl.BlockSpec(memory_space=pltpu.HBM)],
        out_specs=(whole, pl.BlockSpec(memory_space=pltpu.SMEM), pl.BlockSpec(memory_space=pltpu.SMEM)),
        scratch_shapes=[
            pltpu.VMEM((B, D), F32),
            pltpu.SemaphoreType.DMA,
            pltpu.VMEM((2, 16, B, D), BF16),
            pltpu.VMEM((D, 32 * B), BF16),
            pltpu.VMEM((8, D, B), BF16),
            pltpu.VMEM((8, D, B), F32),
            pltpu.VMEM((8, 32 * B, B), BF16),
            pltpu.VMEM((64, B), F32),
            pltpu.VMEM((64, B), F32),
            pltpu.VMEM((8, MSG, B), BF16),
            pltpu.VMEM((8, MSG, B), BF16),
            pltpu.VMEM((20, 8, 128), F32),
            pltpu.SemaphoreType.DMA((NUM_GROUPS,)),
            pltpu.SemaphoreType.DMA((NUM_GROUPS,)),
        ],
        compiler_params=pltpu.CompilerParams(
            collective_id=0, has_side_effects=True, vmem_limit_bytes=56 * 2**20),
        name="uniformity",
    )(embeddings)
    return grad * factor.reshape(()), loss.reshape(())


def solution(mesh):
    return jax.shard_map(
        per_device,
        mesh=mesh,
        in_specs=(P(("tour", "team"), None),),
        out_specs=(P(("tour", "team"), None), P()),
        check_vma=False,
    )
```

```python
import math

import jax
import jax.numpy as jnp
from jax import lax
from jax.experimental import pallas as pl
from jax.experimental.pallas import tpu as pltpu
from jax.sharding import PartitionSpec as P

F32, BF16 = jnp.float32, jnp.bfloat16
MESH = pl.DeviceIdType.MESH
SCALE = 4.0 / math.log(2.0)
SHIFT = math.exp(-4.0)
NX, NY, NZ = 4, 4, 8
D, B = 128, 256
H = B // 2
SPAN = 200.0
MSG = D + 16
LO, HI, ALL = pl.ds(0, H), pl.ds(H, H), pl.ds(0, B)

OFFSETS = (0, 1, -1, 2, -2, 3, -3, 4)
SLOT = {o: p for p, o in enumerate(OFFSETS)}
CHIPS = ((0, 0), (1, 0), (3, 0), (0, 1), (0, 3), (2, 0), (0, 2), (1, 1), (1, 3), (3, 1), (3, 3),
         (1, 2), (3, 2), (2, 1), (2, 3), (2, 2))
PLACE = {chip: k for k, chip in enumerate(CHIPS)}
GROUPS = ((0, 0, 5), (1, 0, 5), (0, 5, 7), (1, 5, 7), (0, 7, 11), (1, 7, 11), (0, 11, 15), (1, 11, 15), (0, 15, 16),
          (1, 15, 16))
EVENTS = (("rows1", 3.1), ("cols1", 3.1), ("cols2", 5.2), ("sib1", 5.2), ("rows2", 7.4), ("cols3", 7.4), ("sib2", 7.4),
          ("rows4", 8.9), ("sib3", 8.9), ("cols4", 10.0), ("cols5", 10.0), ("rows3", 10.4), ("sib4", 11.5), ("sib5", 11.5))
AT = dict(EVENTS)
GROUP_AT = tuple(AT[e] for e in ("cols1", "sib1", "cols2", "sib2", "cols3", "sib3", "cols4", "sib4",
                                "cols5", "sib5"))
ROW_AT = {0: 0.0, 1: AT["rows1"], -1: AT["rows1"], 2: AT["rows2"], -2: AT["rows2"], 3: AT["rows3"], -3: AT["rows3"],
          4: AT["rows4"]}
SCORE_US, PULL_US = 0.041, 0.020


def plan():
    events = list(EVENTS)
    n = len(GROUPS)
    goals = [(kind, o, g) for o in (4, 3, -3) for kind in "SP" for g in range(n)]
    goals += [("S", o, g) for g in range(n) for o in (0, 1, 2)]
    for o in (2, 1):
        goals += [("S", -o, g) for g in range(n)]
        goals += [("P", s * o, g) for s in (-1, 1) for g in range(n)]
    goals += [("P", 0, g) for g in range(n)]
    out, done, now = [], set(), 0.0
    todo = list(goals)

    def finish(kind, offsets):
        return all((kind, o, g) in done for o in offsets for g in range(n))

    after = [("total", lambda: finish("S", (0, 1, 2, 3, 4)))]
    after += [("send4", lambda: finish("P", (4,)))]
    after += [("send3", lambda: finish("P", (3,))), ("send-3", lambda: finish("P", (-3,)))]
    after += [("send1", lambda: finish("P", (1,))), ("send-1", lambda: finish("P", (-1,)))]
    ready2 = lambda o: finish("P", (o,)) and now >= sent.get("send-3", 1e9) + 3.2
    after += [("send2", lambda: ready2(2) and ready2(-2))]
    sent = {}
    while todo or events or after:
        while events and events[0][1] <= now:
            out.append((events.pop(0)[0],))
            now += 0.05
        for item in list(after):
            if item[1]():
                out.append((item[0],))
                sent[item[0]] = now
                after.remove(item)
                if item[0] == "total":
                    events.append(("plane", now + 5.5))
        pick = None
        for task in todo:
            kind, o, g = task
            if kind == "S":
                if max(GROUP_AT[g], ROW_AT[o]) <= now:
                    pick = task
                    break
            elif ("S", o, g) in done:
                pick = task
                break
        if pick is None:
            now += 0.05
            continue
        todo.remove(pick)
        done.add(pick)
        out.append(pick)
        core, a, b = GROUPS[pick[2]]
        now += (b - a) * (SCORE_US if pick[0] == "S" else PULL_US)
    return out


def dot(a, b):
    return lax.dot_general(a, b, (((1,), (0,)), ((), ())), preferred_element_type=F32)


def encode(x, msg, cols):
    top = (jnp.max(jnp.abs(x), axis=0, keepdims=True) * 1.01 + 1e-30).astype(BF16)
    y = jnp.exp2(jnp.abs(x) * (SPAN / top.astype(F32)) - SPAN / 2)
    msg[0:D, cols] = jnp.where(x < 0, -y, y).astype(BF16)
    msg[D:MSG, cols] = jnp.broadcast_to(top, (MSG - D, x.shape[1]))


def decode(msg, cols):
    y = msg[0:D, cols].astype(F32)
    top = msg[D:MSG, cols].astype(F32)[0:1]
    x = (jnp.log(jnp.abs(y)) * (1.0 / math.log(2.0)) + SPAN / 2) * (top * (1.0 / SPAN))
    return jnp.where(y < 0, -x, x)


class Net:
    def __init__(self, send, recv):
        t, m = lax.axis_index("tour"), lax.axis_index("team")
        self.z = (t // 4) * 2 + (m // 2) % 2
        self.x, self.y, self.c = t % 4, m // 4, m % 2
        self.send, self.recv, self.groups, self.known = send, recv, [], {}

    def step(self, axis, d, n):
        if (axis, d) not in self.known:
            v = getattr(self, axis) + d
            v = jnp.where(v >= n, v - n, v) if d else v
            self.known[axis, d] = (v // 2, v % 2) if axis == "z" else v
        return self.known[axis, d]

    def at(self, dx=0, dy=0, dz=0, dc=0):
        z = self.step("z", dz % NZ, NZ)
        return (z[0] * 4 + self.step("x", dx % NX, NX),
                self.step("y", dy % NY, NY) * 4 + z[1] * 2 + self.step("c", dc, 2))


class Group:
    def __init__(self, net, size, *copies):
        i = len(net.groups)
        net.groups.append(self)
        sems = dict(send_sem=net.send.at[i], recv_sem=net.recv.at[i], device_id_type=MESH)
        self.copies = [
            pltpu.make_async_remote_copy(src_ref=a, dst_ref=b, device_id=net.at(**where), **sems) for a, b, where in copies]
        self.all = pltpu.make_async_remote_copy(src_ref=size, dst_ref=size, device_id=net.at(dc=1), **sems)

    def start(self):
        for c in self.copies:
            c.start()

    def wait_recv(self):
        self.all.wait_recv()

    def wait_send(self):
        self.all.wait_send()


NUM_GROUPS = 4 + 5 + 6 + 6 + 2


def kernel(emb_hbm, out_ref, loss_ref, emb_ref, fetched, cols, colt, rowt, acc, w, once, twice, mo, mi, sums, send, recv):
    net = Net(send, recv)
    line = [(dz, dc) for dz in range(NZ) for dc in range(2) if (dz, dc) != (0, 0)]
    plane = [(dx, dy) for dx in range(NX) for dy in range(NY) if (dx, dy) != (0, 0)]

    barrier = pltpu.get_barrier_semaphore()
    for dz, dc in line:
        pl.semaphore_signal(barrier, inc=1, device_id=net.at(dz=dz, dc=dc), device_id_type=MESH)
    for dx, dy in plane:
        pl.semaphore_signal(barrier, inc=1, device_id=net.at(dx=dx, dy=dy), device_id_type=MESH)

    fetch = pltpu.make_async_copy(emb_hbm, emb_ref, fetched)
    fetch.start()

    row = lambda o: rowt.at[SLOT[o]]
    rows1 = Group(net, rowt.at[1:3], (row(0), row(-1), dict(dz=1)), (row(0), row(1), dict(dz=-1)))
    rows2 = Group(net, rowt.at[3:5], (row(-1), row(-2), dict(dz=1)), (row(1), row(2), dict(dz=-1)))
    rows3 = Group(net, rowt.at[5:7], (row(-1), row(-3), dict(dz=2)), (row(1), row(3), dict(dz=-2)))
    rows4 = Group(net, row(4), (row(0), row(4), dict(dz=4)))
    place = lambda dx, dy: PLACE[dx % NX, dy % NY]
    along = lambda dx, dy: (cols.at[0, 0], cols.at[0, place(-dx, -dy)], dict(dx=dx, dy=dy))
    by_y = lambda a, b, s: (cols.at[0, place(a, 0), s], cols.at[0, place(a, -b), s], dict(dy=b))
    by_x = lambda a, b, s: (cols.at[0, place(0, a), s], cols.at[0, place(-b, a), s], dict(dx=b))
    cols1 = Group(net, cols.at[0, 1:5], along(1, 0), along(3, 0), along(0, 1), along(0, 3))
    cols2 = Group(net, cols.at[0, 5:7], along(2, 0), along(0, 2))
    cols3 = Group(net, cols.at[0, 7:11], *[f(a, b, s) for b in (1, 3) for a in (1, 3) for f, s in ((by_y, LO), (by_x, HI))])
    cols4 = Group(net, cols.at[0, 11:15], *[f(a, 2, ALL) for a in (1, 3) for f in (by_y, by_x)])
    cols5 = Group(net, cols.at[0, 15], by_y(2, 2, LO), by_x(2, 2, HI))
    sib = [Group(net, cols.at[1, a:b], (cols.at[0, a:b], cols.at[1, a:b], dict(dc=1)))
           for a, b in ((0, 1), (1, 5), (5, 7), (7, 11), (11, 15), (15, 16))]
    msg = lambda o: mo.at[SLOT[o]]
    far = Group(net, mi.at[0], (msg(4).at[:, LO], mi.at[0, :, LO], dict(dz=2)), (msg(4).at[:, HI], mi.at[0, :, HI], dict(dz=-2)))
    third = {3: Group(net, mi.at[1], (msg(3), mi.at[1], dict(dz=1))), -3: Group(net, mi.at[2], (msg(-3), mi.at[2], dict(dz=-1)))}
    second = Group(net, mi.at[3:5], (msg(2), mi.at[3], dict(dz=2)), (msg(-2), mi.at[4], dict(dz=-2)))
    first = {1: Group(net, mi.at[5], (msg(1), mi.at[5], dict(dz=1))), -1: Group(net, mi.at[6], (msg(-1), mi.at[6], dict(dz=-1)))}
    tell_line = Group(net, sums.at[1:16], *[(sums.at[0], sums.at[1 + i], dict(dz=dz, dc=dc)) for i, (dz, dc) in enumerate(line)])
    tell_plane = Group(
        net, sums.at[17:32], *[(sums.at[16], sums.at[17 + i], dict(dx=dx, dy=dy)) for i, (dx, dy) in enumerate(plane)])

    fetch.wait()
    emb = emb_ref[...]
    inv_norm = lax.rsqrt(jnp.sum(emb * emb, axis=1, keepdims=True) + 1e-06)
    direction = emb * inv_norm
    own = direction.astype(BF16)
    wide = own.astype(F32)
    cols[0, 0] = own
    rowt[0] = wide.T.astype(BF16)
    self_weight = jnp.exp(4.0 * jnp.sum(wide * wide, axis=1, keepdims=True) - 4.0)
    once[...] = jnp.zeros_like(once)
    twice[...] = jnp.zeros_like(twice)
    pl.semaphore_wait(barrier, len(line) + len(plane))

    for c in (rows1, cols1, cols2, rows4, sib[0]):
        c.start()

    turned, begun = set(), set()

    def scores(o, g):
        core, a, b = GROUPS[g]
        n = (b - a) * B
        r = (core * 16 + a) * B
        e = jnp.exp2(dot(cols[core, a:b].reshape(n, D), rowt[SLOT[o]]) * SCALE)
        if o >= 0:
            total = once if o in (0, 4) else twice
            total[...] += jnp.sum(e.reshape(n // 64, 64, B), axis=0)
        w[SLOT[o], r:r + n] = e.astype(BF16)

    def pull(o, g):
        core, a, b = GROUPS[g]
        n = (b - a) * B
        r = (core * 16 + a) * B
        if g not in turned:
            turned.add(g)
            for k in range(a, b):
                s = (core * 16 + k) * B
                colt[:, s:s + B] = cols[core, k].astype(F32).T.astype(BF16)
        p = dot(colt[:, r:r + n], w[SLOT[o], r:r + n])
        if o in begun:
            acc[SLOT[o]] += p
        else:
            begun.add(o)
            acc[SLOT[o]] = p

    def event(name):
        if name == "rows1":
            rows1.wait_recv()
            rows2.start()
            rows3.start()
        elif name.startswith("rows"):
            {"rows2": rows2, "rows3": rows3, "rows4": rows4}[name].wait_recv()
        elif name.startswith("cols"):
            k = int(name[4:])
            (cols1, cols2, cols3, cols4, cols5)[k - 1].wait_recv()
            sib[k].start()
            if k == 1:
                cols3.start()
                cols4.start()
            if k == 2:
                cols5.start()
        elif name.startswith("sib"):
            sib[int(name[3:])].wait_recv()
            if name == "sib1":
                sib[0].wait_recv()
        elif name == "total":
            local = (2.0 * jnp.sum(twice[...]) + jnp.sum(once[...])) * SHIFT - jnp.sum(self_weight)
            sums[0] = jnp.full((8, 128), local, F32)
            tell_line.start()
        elif name == "plane":
            tell_line.wait_recv()
            total = sums[0]
            for i in range(len(line)):
                total = total + sums[1 + i]
            sums[16] = total
            tell_plane.start()
        elif name == "send2":
            far.wait_recv()
            for o, half, i in ((2, LO, 1), (-2, HI, 2)):
                third[3 if o > 0 else -3].wait_recv()
                p = SLOT[o]
                acc[p, :, half] += decode(mi.at[0], half)
                encode(acc[p] + decode(mi.at[i], ALL), mo.at[p], ALL)
            second.start()
        else:
            o = int(name[4:])
            encode(acc[SLOT[o]], mo.at[SLOT[o]], ALL)
            {4: far, 3: third[3], -3: third[-3], 1: first[1], -1: first[-1]}[o].start()

    for task in plan():
        if task[0] == "S":
            scores(*task[1:])
        elif task[0] == "P":
            pull(*task[1:])
        else:
            event(task[0])

    pulled = acc[0]
    for c, held in ((first[-1], (6,)), (first[1], (5,)), (second, (3, 4))):
        c.wait_recv()
        for i in held:
            pulled = pulled + decode(mi.at[i], ALL)
    pulled = pulled.T * SHIFT - self_weight * wide
    radial = jnp.sum(direction * pulled, axis=1, keepdims=True)
    grad = inv_norm * (pulled - direction * radial)
    tell_plane.wait_recv()
    total = sums[16]
    for i in range(len(plane)):
        total = total + sums[17 + i]
    rows = float(B * lax.axis_size("tour") * lax.axis_size("team"))
    out_ref[...] = grad * jnp.broadcast_to((rows * rows / 8.0) / total[0:1], (B, D))
    loss_ref[0, 0] = jnp.max(jnp.log(total / (rows * (rows - 1.0))))
    for c in net.groups:
        c.wait_send()


def per_device(embeddings):
    whole = pl.BlockSpec(memory_space=pltpu.VMEM)
    grad, loss = pl.pallas_call(
        kernel,
        out_shape=(pltpu.VMEM((B, D), F32), jax.ShapeDtypeStruct((1, 1), F32)),
        in_specs=[pl.BlockSpec(memory_space=pltpu.HBM)],
        out_specs=(whole, pl.BlockSpec(memory_space=pltpu.SMEM)),
        scratch_shapes=[
            pltpu.VMEM((B, D), F32),
            pltpu.SemaphoreType.DMA,
            pltpu.VMEM((2, 16, B, D), BF16),
            pltpu.VMEM((D, 32 * B), BF16),
            pltpu.VMEM((8, D, B), BF16),
            pltpu.VMEM((8, D, B), F32),
            pltpu.VMEM((8, 32 * B, B), BF16),
            pltpu.VMEM((64, B), F32),
            pltpu.VMEM((64, B), F32),
            pltpu.VMEM((8, MSG, B), BF16),
            pltpu.VMEM((8, MSG, B), BF16),
            pltpu.VMEM((32, 8, 128), F32),
            pltpu.SemaphoreType.DMA((NUM_GROUPS,)),
            pltpu.SemaphoreType.DMA((NUM_GROUPS,)),
        ],
        compiler_params=pltpu.CompilerParams(
            collective_id=0, has_side_effects=True, vmem_limit_bytes=56 * 2**20),
        name="uniformity",
    )(embeddings)
    return grad, loss.reshape(())


def solution(mesh):
    return jax.shard_map(
        per_device,
        mesh=mesh,
        in_specs=(P(("tour", "team"), None),),
        out_specs=(P(("tour", "team"), None), P()),
        check_vma=False,
    )
```
